1024 devices in a mesh: wide: 64 (over z, core), narrow: 16 (over y, x).
Axes of the slice: x: 4, y: 4, z: 32, core: 2. Of those that a mesh axis runs over, the one named last changes fastest.
Arguments:
- grad: bfloat16 [64, 1792, 1024], P('wide', 'narrow'), may hold values from -60 to 60, as said below
- momentum: bfloat16 [64, 2, 1792, 1024], P('wide', None, 'narrow'), may hold values from -6 to 6
- owner: int32 [32], replicated, may hold values from 0 to 63, as said below
Outputs:
- update: bfloat16 [64, 1792, 1024], P('wide', 'narrow')
- new_momentum: bfloat16 [64, 2, 1792, 1024], P('wide', None, 'narrow')
The draws below stay inside these ranges and needn't reach their ends.
Inputs may be any that keep to these rules, and one draw needn't show every extreme that they name: `grad`: finite values. owner[e] is 2e-1, 2e, 2e+1 or 2e+2, taken modulo 2 * 32; no two experts have the same owner.
All inputs are finite; a program needn't handle non-finite values.
Results may differ from the reference program's by a relative error of at most 0.02.
Values may be sent and summed in bfloat16 or wider, within the bound.
A program may use at most 32 MiB of HBM per device.

```python
import jax
import jax.numpy as jnp
from jax import lax

D = 3584
H = 1024
EXPERTS = 32
N_NARROW = 16


def draw_grad(key, part):
    key = jax.random.fold_in(key, 11)
    shape = (2 * EXPERTS, D // 2, H)
    values = jnp.clip(jax.random.normal(jax.random.fold_in(key, 4), shape, jnp.float32), -6.0, 6.0)
    return values.astype(jnp.bfloat16)


def draw_owner(key, part):
    key = jax.random.fold_in(key, 23)
    picks = (jax.random.randint(jax.random.fold_in(key, 1), (EXPERTS,), 0, 4) - 1).astype(jnp.int32)
    others = jax.random.randint(jax.random.fold_in(key, 2), (EXPERTS,), 0, 3).astype(jnp.int32)
    picks = picks.at[0].set(-1)

    def advance(previous, items):
        pick, other = items
        after_one = other
        after_two = jnp.where(other == 0, -1, other).astype(jnp.int32)
        offset = jnp.where(jnp.logical_and(previous == 1, pick == -1), after_one, pick)
        offset = jnp.where(jnp.logical_and(previous == 2, pick == 0), after_two, offset).astype(jnp.int32)
        return (offset, offset)
    unused, offsets = lax.scan(advance, jnp.int32(0), (picks, others))
    offsets = offsets.at[EXPERTS - 1].set(2)
    groups = 2 * EXPERTS
    return ((2 * jnp.arange(EXPERTS, dtype=jnp.int32) + offsets + groups) % groups).astype(jnp.int32)


def shard_levels(rng, shape, cuts, smallest, top_value):
    def one(axis_at, blocks):
        steps = jax.random.uniform(jax.random.fold_in(jax.random.fold_in(rng, 6), axis_at), (blocks,), jnp.float32, smallest / len(cuts), top_value / len(cuts))
        return jnp.repeat(jnp.exp(steps), shape[axis_at] // blocks).reshape((-1,) + (1,) * (len(shape) - axis_at - 1))

    loudness = one(*cuts[0])
    for cut in cuts[1:]:
        loudness = loudness * one(*cut)
    return loudness


def centred(own_key, extent, width, reach, cuts=(), kind=jnp.bfloat16):
    entries = width * jax.random.normal(own_key, extent, jnp.float32)
    if cuts:
        entries = entries * shard_levels(own_key, extent, cuts, -0.22, 0.18)
    return jnp.clip(entries, -reach, reach).astype(kind)


def setup_inputs(seed: int = 0) -> dict:
    keys = jax.random.split(jax.random.key(seed), 4)
    return {
        "grad": draw_grad(jax.random.fold_in(keys[3], 71), 0),
        "momentum": centred(keys[1], (2 * EXPERTS, 2, D // 2, H), 1.0, 6.0, ((0, 64), (2, 16))),
        "owner": draw_owner(jax.random.fold_in(keys[3], 71), 0),
    }


momentum_rate = 0.9
norm_eps = 1e-07

def reference(grad, momentum, owner):
    experts = grad.shape[0] // 2
    half = D // 2
    rows = half // N_NARROW

    def one_expert(items):
        halves, group = items
        stored = momentum[group]
        grad_value = halves.astype(jnp.float32)
        velocity = momentum_rate * stored.astype(jnp.float32) + grad_value
        block = (grad_value + momentum_rate * velocity).astype(jnp.bfloat16)
        pieces = block.reshape(2, N_NARROW, rows, H).transpose(1, 0, 2, 3).reshape(N_NARROW, 2 * rows, H)
        pieces32 = pieces.astype(jnp.float32)
        partial_value = jnp.einsum('nrh,nrk->nhk', pieces32, pieces32, precision=lax.Precision.HIGHEST)
        rounded = lax.optimization_barrier(partial_value.astype(jnp.bfloat16))
        gram = lax.optimization_barrier(jnp.sum(rounded.astype(jnp.float32), axis=0)).astype(jnp.bfloat16)
        trace_sum = jnp.trace(gram.astype(jnp.float32))
        flat = block.reshape(2 * half, H)
        product = jnp.dot(flat, gram, preferred_element_type=jnp.float32)
        factor = jnp.sqrt(jnp.float32(H)) / (jnp.sqrt(trace_sum) + norm_eps)
        result = factor * (1.5 * flat.astype(jnp.float32) - 0.5 * factor * factor * product)
        result = result * jnp.sqrt(jnp.float32(D))
        return (velocity.astype(jnp.bfloat16), result.reshape(2, half, H).astype(jnp.bfloat16))
    states, updates = lax.map(one_expert, (grad.reshape(experts, 2, half, H), owner))
    new_momentum = jnp.zeros_like(momentum).at[owner].set(states)
    update = updates.reshape(2 * experts, half, H)
    return (update, new_momentum)
```

```python
import functools

import jax
import jax.numpy as jnp
from jax import lax
from jax.experimental import pallas as pl
from jax.experimental.pallas import tpu as pltpu
from jax.sharding import PartitionSpec as P

D = 3584
SIDE = 4
TILE = 256

momentum_rate = 0.9
norm_eps = 1e-07

TILES = (
    ((0, 0), (1, 1), (0, 1), (0, 2), (1, 3)),
    ((2, 2), (3, 3), (2, 3), (0, 3), (1, 2)),
)


def kernel(
    planes,
    owner_ref,
    grad_ref,
    mom_ref,
    upd_ref,
    newm_ref,
    g_own,
    g_nb,
    m_loc,
    m_in,
    xf,
    part,
    r1,
    s1,
    r2,
    gram,
    local_sem,
    m_send,
    m_recv,
    g_send,
    g_recv,
    x_send,
    x_recv,
    a_send,
    a_recv,
    b_send,
    b_recv,
    c_send,
    c_recv,
    d_send,
    d_recv,
    e_send,
    e_recv,
):
    rows = grad_ref.shape[1]
    w = lax.axis_index("wide")
    n = lax.axis_index("narrow")
    z, c = w // 2, w % 2
    y, x = n // SIDE, n % SIDE
    up, down = (z + 1) % planes, (z + planes - 1) % planes
    sibling = (z * 2 + 1 - c, n)
    near = jnp.where(c == 0, down, up)

    first = jnp.where(c == 0, x, y)
    second = jnp.where(c == 0, y, x)

    def first_peer(k):
        there = (first + k) % SIDE
        return (w, jnp.where(c == 0, y * SIDE + there, there * SIDE + x))

    def second_peer(k):
        there = (second + k) % SIDE
        return (w, jnp.where(c == 0, there * SIDE + x, y * SIDE + there))

    def remote(src, dst, send, recv, device):
        return pltpu.make_async_remote_copy(
            src_ref=src,
            dst_ref=dst,
            send_sem=send,
            recv_sem=recv,
            device_id=device,
            device_id_type=pl.DeviceIdType.MESH,
        )

    load_m = pltpu.make_async_copy(mom_ref.at[0], m_loc, local_sem.at[0])
    load_g = pltpu.make_async_copy(grad_ref.at[0], g_own.at[c], local_sem.at[1])
    load_m.start()
    load_g.start()

    barrier = pltpu.get_barrier_semaphore()
    partners = [sibling, (near * 2, n), (near * 2 + 1, n), (jnp.where(c == 0, up, down) * 2 + c, n)]
    for k in range(1, SIDE):
        partners += [first_peer(k), second_peer(k)]
    for device in partners:
        pl.semaphore_signal(barrier, inc=1, device_id=device, device_id_type=pl.DeviceIdType.MESH)
    pl.semaphore_wait(barrier, len(partners))

    slot = jnp.where(c == 0, 2, 1)
    m_copies = [
        remote(mom_ref.at[0, 1 - c], m_in.at[0], m_send.at[0], m_recv.at[0], sibling),
        remote(mom_ref.at[0, 0], m_in.at[slot], m_send.at[1], m_recv.at[slot], (near * 2, n)),
        remote(mom_ref.at[0, 1], m_in.at[slot], m_send.at[2], m_recv.at[slot], (near * 2 + 1, n)),
    ]
    for copy in m_copies:
        copy.start()
    load_m.wait()
    load_g.wait()
    for k in range(3):
        remote(m_in.at[k], m_in.at[k], m_send.at[k], m_recv.at[k], sibling).wait_recv()

    offset = (owner_ref[z] - 2 * z + 2 * planes) % (2 * planes)
    mine = pl.ds(pl.multiple_of(c * rows, 16), rows)
    stored = jnp.where(
        offset == c,
        m_loc[c],
        jnp.where(offset == 1 - c, m_in[0], jnp.where(offset == 2, m_in[2], m_in[1])),
    )
    grad_value = g_own[c].astype(jnp.float32)
    velocity = momentum_rate * stored.astype(jnp.float32) + grad_value
    xf[mine, :] = (grad_value + momentum_rate * velocity).astype(jnp.bfloat16)
    x_copy = remote(xf.at[mine], xf.at[mine], x_send, x_recv, sibling)
    x_copy.start()

    g_copies = [
        remote(grad_ref.at[0], g_own.at[c], g_send.at[0], g_recv.at[0], sibling),
        remote(grad_ref.at[0], g_nb.at[c], g_send.at[1], g_recv.at[1 + c], (up * 2, n)),
        remote(grad_ref.at[0], g_nb.at[c], g_send.at[2], g_recv.at[1 + c], (down * 2 + 1, n)),
    ]
    for copy in g_copies:
        copy.start()
    x_copy.wait()

    for t in range(5):
        i = jnp.where(c == 0, TILES[0][t][0], TILES[1][t][0])
        j = jnp.where(c == 0, TILES[0][t][1], TILES[1][t][1])
        left = xf[:, pl.ds(pl.multiple_of(i * TILE, TILE), TILE)]
        right = xf[:, pl.ds(pl.multiple_of(j * TILE, TILE), TILE)]
        tile = lax.dot_general(left, right, (((0,), (0,)), ((), ())), preferred_element_type=jnp.float32)
        part[t * TILE : (t + 1) * TILE, :] = tile.astype(jnp.bfloat16)

    total = part.shape[0]
    quarter = total // SIDE
    piece = quarter // SIDE

    def quarter_at(k):
        return pl.ds(pl.multiple_of(k * quarter, 16), quarter)

    def piece_at(k):
        return pl.ds(pl.multiple_of(k * piece, 16), piece)

    a_copies = []
    for k in (2, 1, 3):
        there = (first + k) % SIDE
        copy = remote(part.at[quarter_at(there)], r1.at[k - 1], a_send.at[k - 1], a_recv.at[k - 1], first_peer(k))
        copy.start()
        a_copies.append(copy)
    acc = part[quarter_at(first), :].astype(jnp.float32)
    for copy in a_copies:
        copy.wait_recv()
    for k in range(3):
        acc = acc + r1[k].astype(jnp.float32)
    s1[...] = acc.astype(jnp.bfloat16)

    b_copies = []
    for k in (2, 1, 3):
        there = (second + k) % SIDE
        copy = remote(s1.at[piece_at(there)], r2.at[k - 1], b_send.at[k - 1], b_recv.at[k - 1], second_peer(k))
        copy.start()
        b_copies.append(copy)
    acc = s1[piece_at(second), :].astype(jnp.float32)
    for copy in b_copies:
        copy.wait_recv()
    for k in range(3):
        acc = acc + r2[k].astype(jnp.float32)

    own = pl.ds(pl.multiple_of(first * quarter + second * piece, 16), piece)
    gram[c, own, :] = acc.astype(jnp.bfloat16)
    c_copies = []
    for k in (2, 1, 3):
        copy = remote(gram.at[c, own], gram.at[c, own], c_send.at[k - 1], c_recv.at[k - 1], second_peer(k))
        copy.start()
        c_copies.append(copy)

    for copy in g_copies:
        copy.wait_send()
    for k in range(3):
        remote(g_own.at[0], g_own.at[0], g_send.at[k], g_recv.at[k], sibling).wait_recv()
    live_main = owner_ref[z] == w
    live_near = owner_ref[near] == w
    for h in range(2):
        arrived = jnp.where(live_main, g_own[h], g_nb[h]).astype(jnp.float32)
        state = momentum_rate * m_loc[h].astype(jnp.float32) + arrived
        newm_ref[0, h] = jnp.where(jnp.logical_or(live_main, live_near), state, 0.0).astype(jnp.bfloat16)

    for copy in c_copies:
        copy.wait_recv()
    d_copies = []
    for k in (2, 1, 3):
        here = quarter_at(first)
        copy = remote(gram.at[c, here], gram.at[c, here], d_send.at[k - 1], d_recv.at[k - 1], first_peer(k))
        copy.start()
        d_copies.append(copy)

    e_copies = []
    for k in (0, 1, 3, 2):
        here = quarter_at((first + SIDE - k) % SIDE)
        if k:
            remote(gram.at[c, here], gram.at[c, here], d_send.at[k - 1], d_recv.at[k - 1], sibling).wait_recv()
        copy = remote(gram.at[c, here], gram.at[c, here], e_send.at[k], e_recv.at[k], sibling)
        copy.start()
        e_copies.append(copy)
    for copy in e_copies:
        copy.wait_recv()

    row_ids = lax.broadcasted_iota(jnp.int32, (TILE, TILE), 0)
    col_ids = lax.broadcasted_iota(jnp.int32, (TILE, TILE), 1)
    diagonal = jnp.zeros((TILE, TILE), jnp.float32)
    place = {}
    for core in range(2):
        for t, pair in enumerate(TILES[core]):
            place[pair] = (core, t)
            if pair[0] == pair[1]:
                tile = gram[core, t * TILE : (t + 1) * TILE, :].astype(jnp.float32)
                diagonal = diagonal + jnp.where(row_ids == col_ids, tile, 0.0)
    trace_sum = jnp.sum(jnp.sum(diagonal, axis=0, keepdims=True), axis=1, keepdims=True)
    width = grad_ref.shape[2]
    factor = jnp.sqrt(jnp.float32(width)) / (jnp.sqrt(trace_sum) + norm_eps)
    tiles = width // TILE
    for j in range(tiles):
        product = jnp.zeros((rows, TILE), jnp.float32)
        for i in range(tiles):
            core, t = place[(min(i, j), max(i, j))]
            tile = gram[core, t * TILE : (t + 1) * TILE, :]
            dims = (((1,), (0,)), ((), ())) if i <= j else (((1,), (1,)), ((), ()))
            product = product + lax.dot_general(
                xf[mine, i * TILE : (i + 1) * TILE], tile, dims, preferred_element_type=jnp.float32
            )
        block = xf[mine, j * TILE : (j + 1) * TILE].astype(jnp.float32)
        result = factor * (1.5 * block - 0.5 * factor * factor * product)
        upd_ref[0, :, j * TILE : (j + 1) * TILE] = (result * jnp.sqrt(jnp.float32(D))).astype(jnp.bfloat16)

    for copy in m_copies + a_copies + b_copies + c_copies + d_copies + e_copies:
        copy.wait_send()


def solution(mesh):
    planes = mesh.shape["wide"] // 2

    def body(grad, momentum, owner):
        rows, width = grad.shape[1:]
        tall = 5 * TILE
        kind = jnp.bfloat16
        dma = pltpu.SemaphoreType.DMA
        return pl.pallas_call(
            functools.partial(kernel, planes),
            out_shape=(
                jax.ShapeDtypeStruct(grad.shape, kind),
                jax.ShapeDtypeStruct(momentum.shape, kind),
            ),
            in_specs=[
                pl.BlockSpec(memory_space=pltpu.SMEM),
                pl.BlockSpec(memory_space=pl.ANY),
                pl.BlockSpec(memory_space=pl.ANY),
            ],
            out_specs=(
                pl.BlockSpec(memory_space=pltpu.VMEM),
                pl.BlockSpec(memory_space=pltpu.VMEM),
            ),
            scratch_shapes=[
                pltpu.VMEM((2, rows, width), kind),
                pltpu.VMEM((2, rows, width), kind),
                pltpu.VMEM((2, rows, width), kind),
                pltpu.VMEM((3, rows, width), kind),
                pltpu.VMEM((2 * rows, width), kind),
                pltpu.VMEM((tall, TILE), kind),
                pltpu.VMEM((3, tall // SIDE, TILE), kind),
                pltpu.VMEM((tall // SIDE, TILE), kind),
                pltpu.VMEM((3, tall // SIDE // SIDE, TILE), kind),
                pltpu.VMEM((2, tall, TILE), kind),
                dma((2,)),
                dma((3,)), dma((3,)),
                dma((3,)), dma((3,)),
                dma, dma,
                dma((3,)), dma((3,)),
                dma((3,)), dma((3,)),
                dma((3,)), dma((3,)),
                dma((3,)), dma((3,)),
                dma((4,)), dma((4,)),
            ],
            compiler_params=pltpu.CompilerParams(
                collective_id=0, has_side_effects=True, vmem_limit_bytes=40 * 1024 * 1024
            ),
        )(owner, grad, momentum)

    return jax.shard_map(
        body,
        mesh=mesh,
        in_specs=(P("wide", "narrow", None), P("wide", None, "narrow", None), P()),
        out_specs=(P("wide", "narrow", None), P("wide", None, "narrow", None)),
        check_vma=False,
    )
```

```python
import functools

import jax
import jax.numpy as jnp
from jax import lax
from jax.experimental import pallas as pl
from jax.experimental.pallas import tpu as pltpu
from jax.sharding import PartitionSpec as P

D = 3584
SIDE = 4
TILE = 256
VMEM_LIMIT = 60 * 1024 * 1024

momentum_rate = 0.9
norm_eps = 1e-07

TILES = (
    ((0, 0), (1, 1), (1, 2), (0, 3), (2, 3)),
    ((0, 1), (0, 2), (2, 2), (1, 3), (3, 3)),
)
ROUNDS = len(TILES[0])


def kernel(
    planes,
    owner_hbm,
    grad_ref,
    mom_ref,
    upd_hbm,
    newm_hbm,
    owner_ref,
    upd_ref,
    newm_ref,
    g_own,
    g_nb,
    m_loc,
    m_in,
    xf,
    part,
    r1,
    s1,
    r2,
    gram,
    far_sem,
    local_sem,
    out_sem,
    m_send,
    m_recv,
    g_send,
    g_recv,
    x_send,
    x_recv,
    a_send,
    a_recv,
    b_send,
    b_recv,
    d_send,
    d_recv,
    e_send,
    e_recv,
):
    rows, width = grad_ref.shape[1:]
    columns = width // TILE
    strip = TILE // SIDE
    w = lax.axis_index("wide")
    n = lax.axis_index("narrow")
    z, c = w // 2, w % 2
    y, x = n // SIDE, n % SIDE
    up, down = (z + 1) % planes, (z + planes - 1) % planes
    sibling = (z * 2 + 1 - c, n)
    near = jnp.where(c == 0, down, up)

    first = jnp.where(c == 0, x, y)
    second = jnp.where(c == 0, y, x)

    def first_peer(k):
        there = (first + k) % SIDE
        return (w, jnp.where(c == 0, y * SIDE + there, there * SIDE + x))

    def second_peer(k):
        there = (second + k) % SIDE
        return (w, jnp.where(c == 0, there * SIDE + x, y * SIDE + there))

    def remote(src, dst, send, recv, device):
        return pltpu.make_async_remote_copy(
            src_ref=src,
            dst_ref=dst,
            send_sem=send,
            recv_sem=recv,
            device_id=device,
            device_id_type=pl.DeviceIdType.MESH,
        )

    sent = []

    def push(*args):
        copy = remote(*args)
        copy.start()
        sent.append(copy)

    def arrived(ref, recv):
        remote(ref, ref, recv, recv, sibling).wait_recv()

    load_m = pltpu.make_async_copy(mom_ref.at[0], m_loc, local_sem.at[0])
    load_g = pltpu.make_async_copy(grad_ref.at[0], g_own.at[c], local_sem.at[1])
    load_o = pltpu.make_async_copy(owner_hbm, owner_ref, local_sem.at[2])
    load_o.start()
    load_m.start()
    load_g.start()

    barrier = pltpu.get_barrier_semaphore()
    partners = [sibling, (near * 2, n), (near * 2 + 1, n), (jnp.where(c == 0, up, down) * 2 + c, n)]
    for k in (1, 3):
        partners += [first_peer(k), second_peer(k)]
    for device in partners:
        pl.semaphore_signal(barrier, inc=1, device_id=device, device_id_type=pl.DeviceIdType.MESH)
    pl.semaphore_wait(barrier, len(partners))
    pl.semaphore_signal(far_sem.at[0], inc=1, device_id=first_peer(3), device_id_type=pl.DeviceIdType.MESH)
    pl.semaphore_signal(far_sem.at[1], inc=1, device_id=second_peer(3), device_id_type=pl.DeviceIdType.MESH)

    slot = jnp.where(c == 0, 2, 1)

    def lanes(j):
        return slice(j * TILE, (j + 1) * TILE)

    for j in range(columns):
        push(mom_ref.at[0, 0, :, lanes(j)], m_in.at[j, slot], m_send.at[1, j], m_recv.at[j, slot], (near * 2, n))
        push(mom_ref.at[0, 1, :, lanes(j)], m_in.at[j, slot], m_send.at[2, j], m_recv.at[j, slot], (near * 2 + 1, n))
        push(mom_ref.at[0, 1 - c, :, lanes(j)], m_in.at[j, 0], m_send.at[0, j], m_recv.at[j, 0], sibling)
    load_o.wait()
    load_m.wait()
    load_g.wait()

    offset = (owner_ref[z] - 2 * z + 2 * planes) % (2 * planes)
    mine = pl.ds(pl.multiple_of(c * rows, 16), rows)
    other = pl.ds(pl.multiple_of((1 - c) * rows, 16), rows)

    def make_x(j):
        for k in range(3):
            arrived(m_in.at[j, k], m_recv.at[j, k])
        stored = jnp.where(
            offset == c,
            m_loc[c, :, lanes(j)],
            jnp.where(offset == 1 - c, m_in[j, 0], jnp.where(offset == 2, m_in[j, 2], m_in[j, 1])),
        )
        grad_value = g_own[c, :, lanes(j)].astype(jnp.float32)
        velocity = momentum_rate * stored.astype(jnp.float32) + grad_value
        xf[j, mine, :] = (grad_value + momentum_rate * velocity).astype(jnp.bfloat16)
        push(xf.at[j, mine], xf.at[j, mine], x_send.at[j], x_recv.at[j], sibling)
        arrived(xf.at[j, other], x_recv.at[j])

    def strip_of(k):
        return pl.ds(pl.multiple_of(k * strip, 16), strip)

    def make_tile(r):
        i = jnp.where(c == 0, TILES[0][r][0], TILES[1][r][0])
        j = jnp.where(c == 0, TILES[0][r][1], TILES[1][r][1])
        tile = lax.dot_general(xf[i], xf[j], (((0,), (0,)), ((), ())), preferred_element_type=jnp.float32)
        part[r] = tile.astype(jnp.bfloat16)
        for k in (2, 1, 3):
            there = (first + k) % SIDE
            push(part.at[r, strip_of(there)], r1.at[r, k - 1], a_send.at[r, k - 1], a_recv.at[r, k - 1], first_peer(k))

    def sum_first(r):
        acc = part[r, strip_of(first), :].astype(jnp.float32)
        for k in range(3):
            arrived(r1.at[r, k], a_recv.at[r, k])
        for k in range(3):
            acc = acc + r1[r, k].astype(jnp.float32)
        s1[r] = acc.astype(jnp.bfloat16)
        for k in (2, 1, 3):
            push(s1.at[r], r2.at[r, k - 1], b_send.at[r, k - 1], b_recv.at[r, k - 1], second_peer(k))

    def sum_second(r):
        acc = s1[r].astype(jnp.float32)
        for k in range(3):
            arrived(r2.at[r, k], b_recv.at[r, k])
        for k in range(3):
            acc = acc + r2[r, k].astype(jnp.float32)
        own = strip_of(first)
        gram[c, r, own, :] = acc.astype(jnp.bfloat16)
        for k in (2, 1, 3):
            push(gram.at[c, r, own], gram.at[c, r, own], d_send.at[r, k - 1], d_recv.at[r, k - 1], first_peer(k))

    def pass_tile(r):
        for k in range(1, SIDE):
            there = strip_of((first + SIDE - k) % SIDE)
            arrived(gram.at[c, r, there], d_recv.at[r, k - 1])
        push(gram.at[c, r], gram.at[c, r], e_send.at[r], e_recv.at[r], sibling)

    stored_out = []

    def store(src, dst, sem):
        copy = pltpu.make_async_copy(src, dst, sem)
        copy.start()
        stored_out.append(copy)

    def new_momentum(h):
        live_main = owner_ref[z] == w
        live_near = owner_ref[near] == w
        kept = jnp.where(live_main, g_own[h], g_nb[h]).astype(jnp.float32)
        state = momentum_rate * m_loc[h].astype(jnp.float32) + kept
        newm_ref[h] = jnp.where(jnp.logical_or(live_main, live_near), state, 0.0).astype(jnp.bfloat16)
        store(newm_ref.at[h], newm_hbm.at[0, h], out_sem.at[h])

    make_x(0)
    make_x(1)
    pl.semaphore_wait(far_sem.at[0], 1)
    pl.semaphore_wait(far_sem.at[1], 1)
    make_tile(0)
    make_x(2)
    make_tile(1)
    make_tile(2)
    make_x(3)
    make_tile(3)
    make_tile(4)

    push(grad_ref.at[0], g_nb.at[c], g_send.at[1], g_recv.at[1 + c], (up * 2, n))
    push(grad_ref.at[0], g_nb.at[c], g_send.at[2], g_recv.at[1 + c], (down * 2 + 1, n))
    push(grad_ref.at[0], g_own.at[c], g_send.at[0], g_recv.at[0], sibling)

    sum_first(0)
    sum_first(1)
    sum_first(2)
    sum_first(3)
    sum_second(0)
    sum_first(4)
    sum_second(1)
    sum_second(2)
    sum_second(3)
    pass_tile(0)
    sum_second(4)
    pass_tile(1)
    arrived(g_own.at[1 - c], g_recv.at[0])
    for h in range(2):
        arrived(g_nb.at[h], g_recv.at[1 + h])
        new_momentum(h)
    pass_tile(2)
    pass_tile(3)
    pass_tile(4)
    for r in range(ROUNDS):
        arrived(gram.at[1 - c, r], e_recv.at[r])

    row_ids = lax.broadcasted_iota(jnp.int32, (TILE, TILE), 0)
    col_ids = lax.broadcasted_iota(jnp.int32, (TILE, TILE), 1)
    diagonal = jnp.zeros((TILE, TILE), jnp.float32)
    place = {}
    for core in range(2):
        for r, pair in enumerate(TILES[core]):
            place[pair] = (core, r)
            if pair[0] == pair[1]:
                diagonal = diagonal + jnp.where(row_ids == col_ids, gram[core, r].astype(jnp.float32), 0.0)
    trace_sum = jnp.sum(jnp.sum(diagonal, axis=0, keepdims=True), axis=1, keepdims=True)
    factor = jnp.sqrt(jnp.float32(width)) / (jnp.sqrt(trace_sum) + norm_eps)
    for j in range(columns):
        product = jnp.zeros((rows, TILE), jnp.float32)
        for i in range(columns):
            core, r = place[(min(i, j), max(i, j))]
            dims = (((1,), (0,)), ((), ())) if i <= j else (((1,), (1,)), ((), ()))
            product = product + lax.dot_general(
                xf[i, mine, :], gram[core, r], dims, preferred_element_type=jnp.float32
            )
        block = xf[j, mine, :].astype(jnp.float32)
        result = factor * (1.5 * block - 0.5 * factor * factor * product)
        upd_ref[j] = (result * jnp.sqrt(jnp.float32(D))).astype(jnp.bfloat16)
        store(upd_ref.at[j], upd_hbm.at[0, :, lanes(j)], out_sem.at[2 + j])

    for copy in sent:
        copy.wait_send()
    for copy in stored_out:
        copy.wait()


def finish(upd_in, newm_in, upd_out, newm_out, upd, newm, load_sem, store_sem):
    halves = newm.shape[0]
    pieces = [(newm_in.at[0, h], newm.at[h], newm_out.at[0, h]) for h in range(halves)]
    pieces.append((upd_in.at[0], upd, upd_out.at[0]))
    loads = [pltpu.make_async_copy(src, held, load_sem.at[i]) for i, (src, held, dst) in enumerate(pieces)]
    stores = [pltpu.make_async_copy(held, dst, store_sem.at[i]) for i, (src, held, dst) in enumerate(pieces)]
    for copy in loads:
        copy.start()
    for load, copy in zip(loads, stores):
        load.wait()
        copy.start()
    for copy in stores:
        copy.wait()


def solution(mesh):
    planes = mesh.shape["wide"] // 2

    def body(grad, momentum, owner):
        rows, width = grad.shape[1:]
        columns = width // TILE
        strip = TILE // SIDE
        kind = jnp.bfloat16
        dma = pltpu.SemaphoreType.DMA
        results = pl.pallas_call(
            functools.partial(kernel, planes),
            out_shape=(
                jax.ShapeDtypeStruct(grad.shape, kind),
                jax.ShapeDtypeStruct(momentum.shape, kind),
            ),
            in_specs=[
                pl.BlockSpec(memory_space=pl.ANY),
                pl.BlockSpec(memory_space=pl.ANY),
                pl.BlockSpec(memory_space=pl.ANY),
            ],
            out_specs=(
                pl.BlockSpec(memory_space=pl.ANY),
                pl.BlockSpec(memory_space=pl.ANY),
            ),
            scratch_shapes=[
                pltpu.SMEM(owner.shape, owner.dtype),
                pltpu.VMEM((columns, rows, TILE), kind),
                pltpu.VMEM((2, rows, width), kind),
                pltpu.VMEM((2, rows, width), kind),
                pltpu.VMEM((2, rows, width), kind),
                pltpu.VMEM((2, rows, width), kind),
                pltpu.VMEM((columns, 3, rows, TILE), kind),
                pltpu.VMEM((columns, 2 * rows, TILE), kind),
                pltpu.VMEM((ROUNDS, TILE, TILE), kind),
                pltpu.VMEM((ROUNDS, 3, strip, TILE), kind),
                pltpu.VMEM((ROUNDS, strip, TILE), kind),
                pltpu.VMEM((ROUNDS, 3, strip, TILE), kind),
                pltpu.VMEM((2, ROUNDS, TILE, TILE), kind),
                pltpu.SemaphoreType.REGULAR((2,)),
                dma((3,)),
                dma((2 + columns,)),
                dma((3, columns)),
                dma((columns, 3)),
                dma((3,)),
                dma((3,)),
                dma((columns,)),
                dma((columns,)),
                dma((ROUNDS, 3)),
                dma((ROUNDS, 3)),
                dma((ROUNDS, 3)),
                dma((ROUNDS, 3)),
                dma((ROUNDS, 3)),
                dma((ROUNDS, 3)),
                dma((ROUNDS,)),
                dma((ROUNDS,)),
            ],
            compiler_params=pltpu.CompilerParams(
                collective_id=0, has_side_effects=True, vmem_limit_bytes=VMEM_LIMIT
            ),
        )(owner, grad, momentum)
        return pl.pallas_call(
            finish,
            out_shape=(
                jax.ShapeDtypeStruct(grad.shape, kind),
                jax.ShapeDtypeStruct(momentum.shape, kind),
            ),
            in_specs=[pl.BlockSpec(memory_space=pl.ANY)] * 2,
            out_specs=(pl.BlockSpec(memory_space=pl.ANY),) * 2,
            scratch_shapes=[
                pltpu.VMEM((rows, width), kind),
                pltpu.VMEM((2, rows, width), kind),
                dma((3,)),
                dma((3,)),
            ],
            compiler_params=pltpu.CompilerParams(vmem_limit_bytes=VMEM_LIMIT),
        )(*results)

    return jax.shard_map(
        body,
        mesh=mesh,
        in_specs=(P("wide", "narrow", None), P("wide", None, "narrow", None), P()),
        out_specs=(P("wide", "narrow", None), P("wide", None, "narrow", None)),
        check_vma=False,
    )
```

```python
import functools

import jax
import jax.numpy as jnp
from jax import lax
from jax.experimental import pallas as pl
from jax.experimental.pallas import tpu as pltpu
from jax.sharding import PartitionSpec as P

D = 3584
SIDE = 4
TILE = 256
VMEM_LIMIT = 60 * 1024 * 1024

momentum_rate = 0.9
norm_eps = 1e-07

TILES = (
    ((0, 0), (1, 1), (1, 2), (0, 3), (2, 3)),
    ((0, 1), (0, 2), (2, 2), (1, 3), (3, 3)),
)
ROUNDS = len(TILES[0])


def kernel(
    planes,
    owner_hbm,
    grad_ref,
    mom_ref,
    upd_hbm,
    newm_hbm,
    owner_ref,
    upd_ref,
    newm_ref,
    g_own,
    g_nb,
    m_loc,
    m_in,
    xf,
    part,
    r1,
    s1,
    r2,
    gram,
    near_sem,
    far_sem,
    local_sem,
    out_sem,
    m_send,
    m_recv,
    g_send,
    g_recv,
    x_send,
    x_recv,
    a_send,
    a_recv,
    b_send,
    b_recv,
    d_send,
    d_recv,
    e_send,
    e_recv,
):
    rows, width = grad_ref.shape[1:]
    columns = width // TILE
    strip = TILE // SIDE
    w = lax.axis_index("wide")
    n = lax.axis_index("narrow")
    z, c = w // 2, w % 2
    y, x = n // SIDE, n % SIDE
    up, down = (z + 1) % planes, (z + planes - 1) % planes
    sibling = (z * 2 + 1 - c, n)
    near = jnp.where(c == 0, down, up)

    first = jnp.where(c == 0, x, y)
    second = jnp.where(c == 0, y, x)

    def first_peer(k):
        there = (first + k) % SIDE
        return (w, jnp.where(c == 0, y * SIDE + there, there * SIDE + x))

    def second_peer(k):
        there = (second + k) % SIDE
        return (w, jnp.where(c == 0, there * SIDE + x, y * SIDE + there))

    def remote(src, dst, send, recv, device):
        return pltpu.make_async_remote_copy(
            src_ref=src,
            dst_ref=dst,
            send_sem=send,
            recv_sem=recv,
            device_id=device,
            device_id_type=pl.DeviceIdType.MESH,
        )

    sent = []

    def push(*args):
        copy = remote(*args)
        copy.start()
        sent.append(copy)

    def arrived(ref, recv):
        remote(ref, ref, recv, recv, sibling).wait_recv()

    load_m = pltpu.make_async_copy(mom_ref.at[0], m_loc, local_sem.at[0])
    load_g = pltpu.make_async_copy(grad_ref.at[0], g_own.at[c], local_sem.at[1])
    load_o = pltpu.make_async_copy(owner_hbm, owner_ref, local_sem.at[2])
    load_o.start()
    load_m.start()
    load_g.start()

    def signal(sem, device):
        pl.semaphore_signal(sem, inc=1, device_id=device, device_id_type=pl.DeviceIdType.MESH)

    barrier = pltpu.get_barrier_semaphore()
    signal(barrier, (jnp.where(c == 0, down * 2, up * 2), n))
    signal(barrier, (down * 2 + 1, n))
    signal(barrier, sibling)
    for k in (1, 3):
        signal(barrier, (z * 2, y * SIDE + (x + k) % SIDE))
        signal(barrier, (z * 2, (y + k) % SIDE * SIDE + x))

    @pl.when(c == 0)
    def _():
        signal(barrier, (up * 2, n))

    pl.semaphore_wait(barrier, jnp.where(c == 0, 12, 3))

    @pl.when(c == 0)
    def _():
        signal(near_sem, sibling)

    slot = jnp.where(c == 0, 2, 1)

    def lanes(j):
        return slice(j * TILE, (j + 1) * TILE)

    for j in range(columns):
        push(mom_ref.at[0, 0, :, lanes(j)], m_in.at[j, slot], m_send.at[1, j], m_recv.at[j, slot], (near * 2, n))
        push(mom_ref.at[0, 1, :, lanes(j)], m_in.at[j, slot], m_send.at[2, j], m_recv.at[j, slot], (near * 2 + 1, n))
        push(mom_ref.at[0, 1 - c, :, lanes(j)], m_in.at[j, 0], m_send.at[0, j], m_recv.at[j, 0], sibling)
    load_o.wait()
    load_m.wait()
    load_g.wait()

    @pl.when(c == 1)
    def _():
        pl.semaphore_wait(near_sem, 1)

    signal(far_sem.at[0], first_peer(3))
    signal(far_sem.at[1], second_peer(3))

    offset = (owner_ref[z] - 2 * z + 2 * planes) % (2 * planes)
    mine = pl.ds(pl.multiple_of(c * rows, 16), rows)
    other = pl.ds(pl.multiple_of((1 - c) * rows, 16), rows)

    def send_gradient():
        push(grad_ref.at[0], g_nb.at[c], g_send.at[1], g_recv.at[1 + c], (up * 2, n))
        push(grad_ref.at[0], g_nb.at[c], g_send.at[2], g_recv.at[1 + c], (down * 2 + 1, n))
        push(grad_ref.at[0], g_own.at[c], g_send.at[0], g_recv.at[0], sibling)

    def make_x(j):
        for k in range(3):
            arrived(m_in.at[j, k], m_recv.at[j, k])
        stored = jnp.where(
            offset == c,
            m_loc[c, :, lanes(j)],
            jnp.where(offset == 1 - c, m_in[j, 0], jnp.where(offset == 2, m_in[j, 2], m_in[j, 1])),
        )
        grad_value = g_own[c, :, lanes(j)].astype(jnp.float32)
        velocity = momentum_rate * stored.astype(jnp.float32) + grad_value
        xf[j, mine, :] = (grad_value + momentum_rate * velocity).astype(jnp.bfloat16)
        push(xf.at[j, mine], xf.at[j, mine], x_send.at[j], x_recv.at[j], sibling)
        if j == columns - 1:
            send_gradient()
        arrived(xf.at[j, other], x_recv.at[j])

    def strip_of(k):
        return pl.ds(pl.multiple_of(k * strip, 16), strip)

    def make_tile(r):
        i = jnp.where(c == 0, TILES[0][r][0], TILES[1][r][0])
        j = jnp.where(c == 0, TILES[0][r][1], TILES[1][r][1])
        tile = lax.dot_general(xf[i], xf[j], (((0,), (0,)), ((), ())), preferred_element_type=jnp.float32)
        part[r] = tile.astype(jnp.bfloat16)
        for k in (2, 1, 3):
            there = (first + k) % SIDE
            push(part.at[r, strip_of(there)], r1.at[r, k - 1], a_send.at[r, k - 1], a_recv.at[r, k - 1], first_peer(k))

    def sum_first(r):
        acc = part[r, strip_of(first), :].astype(jnp.float32)
        for k in range(3):
            arrived(r1.at[r, k], a_recv.at[r, k])
        for k in range(3):
            acc = acc + r1[r, k].astype(jnp.float32)
        s1[r] = acc.astype(jnp.bfloat16)
        for k in (2, 1, 3):
            push(s1.at[r], r2.at[r, k - 1], b_send.at[r, k - 1], b_recv.at[r, k - 1], second_peer(k))

    def sum_second(r):
        acc = s1[r].astype(jnp.float32)
        for k in range(3):
            arrived(r2.at[r, k], b_recv.at[r, k])
        for k in range(3):
            acc = acc + r2[r, k].astype(jnp.float32)
        own = strip_of(first)
        gram[c, r, own, :] = acc.astype(jnp.bfloat16)
        for k in (2, 1, 3):
            push(gram.at[c, r, own], gram.at[c, r, own], d_send.at[r, k - 1], d_recv.at[r, k - 1], first_peer(k))

    def pass_tile(r):
        for k in range(1, SIDE):
            there = strip_of((first + SIDE - k) % SIDE)
            arrived(gram.at[c, r, there], d_recv.at[r, k - 1])
        push(gram.at[c, r], gram.at[c, r], e_send.at[r], e_recv.at[r], sibling)

    stored_out = []

    def store(src, dst, sem):
        copy = pltpu.make_async_copy(src, dst, sem)
        copy.start()
        stored_out.append(copy)

    def new_momentum(h):
        live_main = owner_ref[z] == w
        live_near = owner_ref[near] == w
        kept = jnp.where(live_main, g_own[h], g_nb[h]).astype(jnp.float32)
        state = momentum_rate * m_loc[h].astype(jnp.float32) + kept
        newm_ref[h] = jnp.where(jnp.logical_or(live_main, live_near), state, 0.0).astype(jnp.bfloat16)
        store(newm_ref.at[h], newm_hbm.at[0, h], out_sem.at[h])

    make_x(0)
    make_x(1)
    pl.semaphore_wait(far_sem.at[0], 1)
    pl.semaphore_wait(far_sem.at[1], 1)
    make_tile(0)
    make_x(2)
    make_tile(1)
    make_tile(2)
    make_x(3)
    make_tile(3)
    make_tile(4)

    sum_first(0)
    sum_first(1)
    sum_first(2)
    sum_first(3)
    sum_second(0)
    sum_first(4)
    sum_second(1)
    sum_second(2)
    sum_second(3)
    pass_tile(0)
    sum_second(4)
    pass_tile(1)
    pass_tile(2)
    pass_tile(3)

    for copy in sent[:-2 * SIDE]:
        copy.wait_send()
    del sent[:-2 * SIDE]

    row_ids = lax.broadcasted_iota(jnp.int32, (TILE, TILE), 0)
    col_ids = lax.broadcasted_iota(jnp.int32, (TILE, TILE), 1)
    block = [xf[j, mine, :] for j in range(columns)]
    product = [jnp.zeros((rows, TILE), jnp.float32) for j in range(columns)]
    diagonal = [jnp.zeros((TILE, TILE), jnp.float32)]

    def multiply(core, r):
        i, j = TILES[core][r]
        tile = gram[core, r]
        product[j] = product[j] + lax.dot_general(
            block[i], tile, (((1,), (0,)), ((), ())), preferred_element_type=jnp.float32
        )
        if i == j:
            diagonal[0] = diagonal[0] + jnp.where(row_ids == col_ids, tile.astype(jnp.float32), 0.0)
        else:
            product[i] = product[i] + lax.dot_general(
                block[j], tile, (((1,), (1,)), ((), ())), preferred_element_type=jnp.float32
            )

    for r in range(ROUNDS - 2):
        arrived(gram.at[1 - c, r], e_recv.at[r])
        multiply(0, r)
        multiply(1, r)
    pass_tile(ROUNDS - 1)
    arrived(g_own.at[1 - c], g_recv.at[0])
    for h in range(2):
        arrived(g_nb.at[h], g_recv.at[1 + h])
        new_momentum(h)
    for r in range(ROUNDS - 2, ROUNDS):
        arrived(gram.at[1 - c, r], e_recv.at[r])
        multiply(0, r)
        multiply(1, r)

    trace_sum = jnp.sum(jnp.sum(diagonal[0], axis=0, keepdims=True), axis=1, keepdims=True)
    factor = jnp.sqrt(jnp.float32(width)) / (jnp.sqrt(trace_sum) + norm_eps)
    for j in range(columns):
        result = factor * (1.5 * block[j].astype(jnp.float32) - 0.5 * factor * factor * product[j])
        upd_ref[j] = (result * jnp.sqrt(jnp.float32(D))).astype(jnp.bfloat16)
        store(upd_ref.at[j], upd_hbm.at[0, :, lanes(j)], out_sem.at[2 + j])

    for copy in sent:
        copy.wait_send()
    for copy in stored_out:
        copy.wait()


def finish(upd_in, newm_in, upd_out, newm_out, upd, newm, load_sem, store_sem):
    halves = newm.shape[0]
    pieces = [(newm_in.at[0, h], newm.at[h], newm_out.at[0, h]) for h in range(halves)]
    pieces.append((upd_in.at[0], upd, upd_out.at[0]))
    loads = [pltpu.make_async_copy(src, held, load_sem.at[i]) for i, (src, held, dst) in enumerate(pieces)]
    stores = [pltpu.make_async_copy(held, dst, store_sem.at[i]) for i, (src, held, dst) in enumerate(pieces)]
    for copy in loads:
        copy.start()
    for load, copy in zip(loads, stores):
        load.wait()
        copy.start()
    for copy in stores:
        copy.wait()


def solution(mesh):
    planes = mesh.shape["wide"] // 2

    def body(grad, momentum, owner):
        rows, width = grad.shape[1:]
        columns = width // TILE
        strip = TILE // SIDE
        kind = jnp.bfloat16
        dma = pltpu.SemaphoreType.DMA
        results = pl.pallas_call(
            functools.partial(kernel, planes),
            out_shape=(
                jax.ShapeDtypeStruct(grad.shape, kind),
                jax.ShapeDtypeStruct(momentum.shape, kind),
            ),
            in_specs=[
                pl.BlockSpec(memory_space=pl.ANY),
                pl.BlockSpec(memory_space=pl.ANY),
                pl.BlockSpec(memory_space=pl.ANY),
            ],
            out_specs=(
                pl.BlockSpec(memory_space=pl.ANY),
                pl.BlockSpec(memory_space=pl.ANY),
            ),
            scratch_shapes=[
                pltpu.SMEM(owner.shape, owner.dtype),
                pltpu.VMEM((columns, rows, TILE), kind),
                pltpu.VMEM((2, rows, width), kind),
                pltpu.VMEM((2, rows, width), kind),
                pltpu.VMEM((2, rows, width), kind),
                pltpu.VMEM((2, rows, width), kind),
                pltpu.VMEM((columns, 3, rows, TILE), kind),
                pltpu.VMEM((columns, 2 * rows, TILE), kind),
                pltpu.VMEM((ROUNDS, TILE, TILE), kind),
                pltpu.VMEM((ROUNDS, 3, strip, TILE), kind),
                pltpu.VMEM((ROUNDS, strip, TILE), kind),
                pltpu.VMEM((ROUNDS, 3, strip, TILE), kind),
                pltpu.VMEM((2, ROUNDS, TILE, TILE), kind),
                pltpu.SemaphoreType.REGULAR,
                pltpu.SemaphoreType.REGULAR((2,)),
                dma((3,)),
                dma((2 + columns,)),
                dma((3, columns)),
                dma((columns, 3)),
                dma((3,)),
                dma((3,)),
                dma((columns,)),
                dma((columns,)),
                dma((ROUNDS, 3)),
                dma((ROUNDS, 3)),
                dma((ROUNDS, 3)),
                dma((ROUNDS, 3)),
                dma((ROUNDS, 3)),
                dma((ROUNDS, 3)),
                dma((ROUNDS,)),
                dma((ROUNDS,)),
            ],
            compiler_params=pltpu.CompilerParams(
                collective_id=0, has_side_effects=True, vmem_limit_bytes=VMEM_LIMIT
            ),
        )(owner, grad, momentum)
        return pl.pallas_call(
            finish,
            out_shape=(
                jax.ShapeDtypeStruct(grad.shape, kind),
                jax.ShapeDtypeStruct(momentum.shape, kind),
            ),
            in_specs=[pl.BlockSpec(memory_space=pl.ANY)] * 2,
            out_specs=(pl.BlockSpec(memory_space=pl.ANY),) * 2,
            scratch_shapes=[
                pltpu.VMEM((rows, width), kind),
                pltpu.VMEM((2, rows, width), kind),
                dma((3,)),
                dma((3,)),
            ],
            compiler_params=pltpu.CompilerParams(vmem_limit_bytes=VMEM_LIMIT),
        )(*results)

    return jax.shard_map(
        body,
        mesh=mesh,
        in_specs=(P("wide", "narrow", None), P("wide", None, "narrow", None), P()),
        out_specs=(P("wide", "narrow", None), P("wide", None, "narrow", None)),
        check_vma=False,
    )
```

```python
import functools

import jax
import jax.numpy as jnp
from jax import lax
from jax.experimental import pallas as pl
from jax.experimental.pallas import tpu as pltpu
from jax.sharding import PartitionSpec as P

D = 3584
SIDE = 4
TILE = 256
VMEM_LIMIT = 60 * 1024 * 1024

momentum_rate = 0.9
norm_eps = 1e-07

TILES = (
    ((0, 0), (1, 1), (1, 2), (0, 3), (2, 3)),
    ((0, 1), (0, 2), (2, 2), (1, 3), (3, 3)),
)
ROUNDS = len(TILES[0])


def kernel(
    planes,
    owner_hbm,
    grad_ref,
    mom_ref,
    upd_hbm,
    newm_hbm,
    owner_ref,
    upd_ref,
    newm_ref,
    g_own,
    g_nb,
    m_loc,
    m_in,
    xf,
    part,
    r1,
    s1,
    r2,
    gram,
    near_sem,
    far_sem,
    local_sem,
    out_sem,
    m_send,
    m_recv,
    g_send,
    g_recv,
    x_send,
    x_recv,
    a_send,
    a_recv,
    b_send,
    b_recv,
    d_send,
    d_recv,
    e_send,
    e_recv,
    h_send,
    h_recv,
):
    rows, width = grad_ref.shape[1:]
    columns = width // TILE
    strip = TILE // SIDE
    w = lax.axis_index("wide")
    n = lax.axis_index("narrow")
    z, c = w // 2, w % 2
    y, x = n // SIDE, n % SIDE
    up, down = (z + 1) % planes, (z + planes - 1) % planes
    sibling = (z * 2 + 1 - c, n)
    near = jnp.where(c == 0, down, up)

    first = jnp.where(c == 0, x, y)
    second = jnp.where(c == 0, y, x)

    def first_peer(k):
        there = (first + k) % SIDE
        return (w, jnp.where(c == 0, y * SIDE + there, there * SIDE + x))

    def second_peer(k):
        there = (second + k) % SIDE
        return (w, jnp.where(c == 0, there * SIDE + x, y * SIDE + there))

    def remote(src, dst, send, recv, device):
        return pltpu.make_async_remote_copy(
            src_ref=src,
            dst_ref=dst,
            send_sem=send,
            recv_sem=recv,
            device_id=device,
            device_id_type=pl.DeviceIdType.MESH,
        )

    sent = []

    def push(*args):
        copy = remote(*args)
        copy.start()
        sent.append(copy)

    def arrived(ref, recv):
        remote(ref, ref, recv, recv, sibling).wait_recv()

    load_m = pltpu.make_async_copy(mom_ref.at[0], m_loc, local_sem.at[0])
    load_g = pltpu.make_async_copy(grad_ref.at[0], g_own.at[c], local_sem.at[1])
    load_o = pltpu.make_async_copy(owner_hbm, owner_ref, local_sem.at[2])
    load_o.start()
    load_m.start()
    load_g.start()

    def signal(sem, device):
        pl.semaphore_signal(sem, inc=1, device_id=device, device_id_type=pl.DeviceIdType.MESH)

    barrier = pltpu.get_barrier_semaphore()
    signal(barrier, (jnp.where(c == 0, down * 2, up * 2), n))
    signal(barrier, (down * 2 + 1, n))
    signal(barrier, sibling)
    for k in (1, 3):
        signal(barrier, (z * 2, y * SIDE + (x + k) % SIDE))
        signal(barrier, (z * 2, (y + k) % SIDE * SIDE + x))

    @pl.when(c == 0)
    def _():
        signal(barrier, (up * 2, n))

    pl.semaphore_wait(barrier, jnp.where(c == 0, 12, 3))

    @pl.when(c == 0)
    def _():
        signal(near_sem, sibling)

    slot = jnp.where(c == 0, 2, 1)

    def lanes(j):
        return slice(j * TILE, (j + 1) * TILE)

    for j in range(columns):
        push(mom_ref.at[0, 0, :, lanes(j)], m_in.at[j, slot], m_send.at[1, j], m_recv.at[j, slot], (near * 2, n))
        push(mom_ref.at[0, 1, :, lanes(j)], m_in.at[j, slot], m_send.at[2, j], m_recv.at[j, slot], (near * 2 + 1, n))
        push(mom_ref.at[0, 1 - c, :, lanes(j)], m_in.at[j, 0], m_send.at[0, j], m_recv.at[j, 0], sibling)
    load_o.wait()
    load_m.wait()
    load_g.wait()

    @pl.when(c == 1)
    def _():
        pl.semaphore_wait(near_sem, 1)

    signal(far_sem.at[0], first_peer(3))
    signal(far_sem.at[1], second_peer(3))

    offset = (owner_ref[z] - 2 * z + 2 * planes) % (2 * planes)
    mine = pl.ds(pl.multiple_of(c * rows, 16), rows)
    other = pl.ds(pl.multiple_of((1 - c) * rows, 16), rows)

    def send_gradient():
        push(grad_ref.at[0], g_nb.at[c], g_send.at[1], g_recv.at[1 + c], (up * 2, n))
        push(grad_ref.at[0], g_nb.at[c], g_send.at[2], g_recv.at[1 + c], (down * 2 + 1, n))
        push(grad_ref.at[0], g_own.at[c], g_send.at[0], g_recv.at[0], sibling)

    def make_x(j):
        for k in range(3):
            arrived(m_in.at[j, k], m_recv.at[j, k])
        stored = jnp.where(
            offset == c,
            m_loc[c, :, lanes(j)],
            jnp.where(offset == 1 - c, m_in[j, 0], jnp.where(offset == 2, m_in[j, 2], m_in[j, 1])),
        )
        grad_value = g_own[c, :, lanes(j)].astype(jnp.float32)
        velocity = momentum_rate * stored.astype(jnp.float32) + grad_value
        xf[j, mine, :] = (grad_value + momentum_rate * velocity).astype(jnp.bfloat16)
        push(xf.at[j, mine], xf.at[j, mine], x_send.at[j], x_recv.at[j], sibling)
        if j == columns - 1:
            send_gradient()
        arrived(xf.at[j, other], x_recv.at[j])

    def strip_of(k):
        return pl.ds(pl.multiple_of(k * strip, 16), strip)

    def make_tile(r):
        i = jnp.where(c == 0, TILES[0][r][0], TILES[1][r][0])
        j = jnp.where(c == 0, TILES[0][r][1], TILES[1][r][1])
        tile = lax.dot_general(xf[i], xf[j], (((0,), (0,)), ((), ())), preferred_element_type=jnp.float32)
        part[r] = tile.astype(jnp.bfloat16)
        for k in (2, 1, 3):
            there = (first + k) % SIDE
            push(part.at[r, strip_of(there)], r1.at[r, k - 1], a_send.at[r, k - 1], a_recv.at[r, k - 1], first_peer(k))

    def sum_first(r):
        acc = part[r, strip_of(first), :].astype(jnp.float32)
        for k in range(3):
            arrived(r1.at[r, k], a_recv.at[r, k])
        for k in range(3):
            acc = acc + r1[r, k].astype(jnp.float32)
        s1[r] = acc.astype(jnp.bfloat16)
        for k in (2, 1, 3):
            push(s1.at[r], r2.at[r, k - 1], b_send.at[r, k - 1], b_recv.at[r, k - 1], second_peer(k))

    def sum_second(r):
        acc = s1[r].astype(jnp.float32)
        for k in range(3):
            arrived(r2.at[r, k], b_recv.at[r, k])
        for k in range(3):
            acc = acc + r2[r, k].astype(jnp.float32)
        own = strip_of(first)
        gram[c, r, own, :] = acc.astype(jnp.bfloat16)
        for k in (2, 1, 3):
            push(gram.at[c, r, own], gram.at[c, r, own], d_send.at[r, k - 1], d_recv.at[r, k - 1], first_peer(k))

    def pass_strips(r):
        for k in (0, 1, 3, 2):
            there = strip_of((first + SIDE - k) % SIDE)
            if k:
                arrived(gram.at[c, r, there], d_recv.at[r, k - 1])
            push(gram.at[c, r, there], gram.at[c, r, there], h_send.at[k], h_recv.at[k], sibling)

    def pass_tile(r):
        for k in range(1, SIDE):
            there = strip_of((first + SIDE - k) % SIDE)
            arrived(gram.at[c, r, there], d_recv.at[r, k - 1])
        push(gram.at[c, r], gram.at[c, r], e_send.at[r], e_recv.at[r], sibling)

    stored_out = []

    def store(src, dst, sem):
        copy = pltpu.make_async_copy(src, dst, sem)
        copy.start()
        stored_out.append(copy)

    def new_momentum(h):
        live_main = owner_ref[z] == w
        live_near = owner_ref[near] == w
        kept = jnp.where(live_main, g_own[h], g_nb[h]).astype(jnp.float32)
        state = momentum_rate * m_loc[h].astype(jnp.float32) + kept
        newm_ref[h] = jnp.where(jnp.logical_or(live_main, live_near), state, 0.0).astype(jnp.bfloat16)
        store(newm_ref.at[h], newm_hbm.at[0, h], out_sem.at[h])

    make_x(0)
    make_x(1)
    pl.semaphore_wait(far_sem.at[0], 1)
    pl.semaphore_wait(far_sem.at[1], 1)
    make_tile(0)
    make_x(2)
    make_tile(1)
    make_tile(2)
    make_x(3)
    make_tile(3)
    make_tile(4)

    for r in range(ROUNDS):
        sum_first(r)
    for r in range(ROUNDS):
        sum_second(r)
    pass_tile(0)
    pass_tile(1)
    pass_tile(2)
    pass_tile(3)

    for copy in sent[:-2 * SIDE]:
        copy.wait_send()
    del sent[:-2 * SIDE]

    row_ids = lax.broadcasted_iota(jnp.int32, (TILE, TILE), 0)
    col_ids = lax.broadcasted_iota(jnp.int32, (TILE, TILE), 1)
    block = [xf[j, mine, :] for j in range(columns)]
    product = [jnp.zeros((rows, TILE), jnp.float32) for j in range(columns)]
    diagonal = [jnp.zeros((TILE, TILE), jnp.float32)]

    def multiply(core, r):
        i, j = TILES[core][r]
        tile = gram[core, r]
        product[j] = product[j] + lax.dot_general(
            block[i], tile, (((1,), (0,)), ((), ())), preferred_element_type=jnp.float32
        )
        if i == j:
            diagonal[0] = diagonal[0] + jnp.where(row_ids == col_ids, tile.astype(jnp.float32), 0.0)
        else:
            product[i] = product[i] + lax.dot_general(
                block[j], tile, (((1,), (1,)), ((), ())), preferred_element_type=jnp.float32
            )

    for r in range(ROUNDS - 2):
        arrived(gram.at[1 - c, r], e_recv.at[r])
        multiply(0, r)
        multiply(1, r)
    pass_strips(ROUNDS - 1)
    arrived(g_own.at[1 - c], g_recv.at[0])
    for h in range(2):
        arrived(g_nb.at[h], g_recv.at[1 + h])
        new_momentum(h)
    arrived(gram.at[1 - c, ROUNDS - 2], e_recv.at[ROUNDS - 2])
    multiply(0, ROUNDS - 2)
    multiply(1, ROUNDS - 2)
    for k in range(SIDE):
        there = strip_of((second + SIDE - k) % SIDE)
        arrived(gram.at[1 - c, ROUNDS - 1, there], h_recv.at[k])
    multiply(0, ROUNDS - 1)
    multiply(1, ROUNDS - 1)

    trace_sum = jnp.sum(jnp.sum(diagonal[0], axis=0, keepdims=True), axis=1, keepdims=True)
    factor = jnp.sqrt(jnp.float32(width)) / (jnp.sqrt(trace_sum) + norm_eps)
    for j in range(columns):
        result = factor * (1.5 * block[j].astype(jnp.float32) - 0.5 * factor * factor * product[j])
        upd_ref[j] = (result * jnp.sqrt(jnp.float32(D))).astype(jnp.bfloat16)
        store(upd_ref.at[j], upd_hbm.at[0, :, lanes(j)], out_sem.at[2 + j])

    for copy in sent:
        copy.wait_send()
    for copy in stored_out:
        copy.wait()


def finish(upd_in, newm_in, upd_out, newm_out, upd, newm, load_sem, store_sem):
    halves = newm.shape[0]
    pieces = [(newm_in.at[0, h], newm.at[h], newm_out.at[0, h]) for h in range(halves)]
    pieces.append((upd_in.at[0], upd, upd_out.at[0]))
    loads = [pltpu.make_async_copy(src, held, load_sem.at[i]) for i, (src, held, dst) in enumerate(pieces)]
    stores = [pltpu.make_async_copy(held, dst, store_sem.at[i]) for i, (src, held, dst) in enumerate(pieces)]
    for copy in loads:
        copy.start()
    for load, copy in zip(loads, stores):
        load.wait()
        copy.start()
    for copy in stores:
        copy.wait()


def solution(mesh):
    planes = mesh.shape["wide"] // 2

    def body(grad, momentum, owner):
        rows, width = grad.shape[1:]
        columns = width // TILE
        strip = TILE // SIDE
        kind = jnp.bfloat16
        dma = pltpu.SemaphoreType.DMA
        results = pl.pallas_call(
            functools.partial(kernel, planes),
            out_shape=(
                jax.ShapeDtypeStruct(grad.shape, kind),
                jax.ShapeDtypeStruct(momentum.shape, kind),
            ),
            in_specs=[
                pl.BlockSpec(memory_space=pl.ANY),
                pl.BlockSpec(memory_space=pl.ANY),
                pl.BlockSpec(memory_space=pl.ANY),
            ],
            out_specs=(
                pl.BlockSpec(memory_space=pl.ANY),
                pl.BlockSpec(memory_space=pl.ANY),
            ),
            scratch_shapes=[
                pltpu.SMEM(owner.shape, owner.dtype),
                pltpu.VMEM((columns, rows, TILE), kind),
                pltpu.VMEM((2, rows, width), kind),
                pltpu.VMEM((2, rows, width), kind),
                pltpu.VMEM((2, rows, width), kind),
                pltpu.VMEM((2, rows, width), kind),
                pltpu.VMEM((columns, 3, rows, TILE), kind),
                pltpu.VMEM((columns, 2 * rows, TILE), kind),
                pltpu.VMEM((ROUNDS, TILE, TILE), kind),
                pltpu.VMEM((ROUNDS, 3, strip, TILE), kind),
                pltpu.VMEM((ROUNDS, strip, TILE), kind),
                pltpu.VMEM((ROUNDS, 3, strip, TILE), kind),
                pltpu.VMEM((2, ROUNDS, TILE, TILE), kind),
                pltpu.SemaphoreType.REGULAR,
                pltpu.SemaphoreType.REGULAR((2,)),
                dma((3,)),
                dma((2 + columns,)),
                dma((3, columns)),
                dma((columns, 3)),
                dma((3,)),
                dma((3,)),
                dma((columns,)),
                dma((columns,)),
                dma((ROUNDS, 3)),
                dma((ROUNDS, 3)),
                dma((ROUNDS, 3)),
                dma((ROUNDS, 3)),
                dma((ROUNDS, 3)),
                dma((ROUNDS, 3)),
                dma((ROUNDS,)),
                dma((ROUNDS,)),
                dma((SIDE,)),
                dma((SIDE,)),
            ],
            compiler_params=pltpu.CompilerParams(
                collective_id=0, has_side_effects=True, vmem_limit_bytes=VMEM_LIMIT
            ),
        )(owner, grad, momentum)
        return pl.pallas_call(
            finish,
            out_shape=(
                jax.ShapeDtypeStruct(grad.shape, kind),
                jax.ShapeDtypeStruct(momentum.shape, kind),
            ),
            in_specs=[pl.BlockSpec(memory_space=pl.ANY)] * 2,
            out_specs=(pl.BlockSpec(memory_space=pl.ANY),) * 2,
            scratch_shapes=[
                pltpu.VMEM((rows, width), kind),
                pltpu.VMEM((2, rows, width), kind),
                dma((3,)),
                dma((3,)),
            ],
            compiler_params=pltpu.CompilerParams(vmem_limit_bytes=VMEM_LIMIT),
        )(*results)

    return jax.shard_map(
        body,
        mesh=mesh,
        in_specs=(P("wide", "narrow", None), P("wide", None, "narrow", None), P()),
        out_specs=(P("wide", "narrow", None), P("wide", None, "narrow", None)),
        check_vma=False,
    )
```
